256 devices in a mesh: tm: 64 (over z, y, core), pix: 4 (over x).
Axes of the slice: x: 4, y: 4, z: 8, core: 2. Of those that a mesh axis runs over, the one named last changes fastest.
Arguments:
- frames: bfloat16 [1024, 131072], P('tm', 'pix'), may hold values from -30 to 30, as said below
- band_edges: int32 [65], replicated, may hold values from 0 to 384, as said below
Outputs:
- coherence: float32 [64, 2, 8, 8], P('tm')
The draws below stay inside these ranges and needn't reach their ends.
Inputs may be any that keep to these rules, and one draw needn't show every extreme that they name: `frames`: image intensities with a level of their own in each pixel. Strictly increasing, band_edges[0] = 0 and band_edges[64] = 384; the bands have uneven widths.
All inputs are finite; a program needn't handle non-finite values.
Results may differ from the reference program's by a relative error of at most 0.0096.
Values may be sent and summed in bfloat16 or wider, within the bound.
No kernel may reach another device: no remote copies, remote signals or barrier semaphores. Data moves between devices by JAX's collectives and lax.ppermute only.
A program may use at most 128 MiB of HBM per device.

```python
import math
import jax
import jax.numpy as jnp
from jax import lax

NT = 1024
TAPERS = 8
NB = 384
NBANDS = 64
PIX_DEV = 32768
PIXELS = 131072
N_PIX = 4


def draw_frames(key, part):
    noise_key = jax.random.fold_in(key, 11)
    scale_key = jax.random.fold_in(key, 12)
    level_key = jax.random.fold_in(key, 13)
    noise_part = jnp.clip(jax.random.normal(noise_key, (NT, PIXELS), jnp.float32), -6.0, 6.0)
    scaling = jnp.exp(jax.random.uniform(scale_key, (1, PIXELS), jnp.float32, -0.7, 0.7))
    offset = jax.random.uniform(level_key, (1, PIXELS), jnp.float32, -1.0, 1.0)
    return ((noise_part + offset) * scaling).astype(jnp.bfloat16)


def draw_band_edges(key, part):
    cut_points = jax.random.permutation(jax.random.fold_in(key, 21), NB - 1)[:NBANDS - 1].astype(jnp.int32) + 1
    cut_points = jnp.sort(cut_points)
    return jnp.concatenate([jnp.zeros((1,), jnp.int32), cut_points, jnp.full((1,), NB, jnp.int32)])


def setup_inputs(seed: int = 0) -> dict:
    keys = jax.random.split(jax.random.key(seed), 3)
    return {
        "frames": draw_frames(jax.random.fold_in(keys[2], 71), 0),
        "band_edges": draw_band_edges(jax.random.fold_in(keys[2], 71), 0),
    }


def transform_table(length, bins, tapers):
    frame_ids = jnp.arange(length, dtype=jnp.int32)
    bin_ids = jnp.arange(bins, dtype=jnp.int32)
    phase = (bin_ids[:, None] * frame_ids[None, :] % length).astype(jnp.float32) * (2.0 * math.pi / length)
    orders = jnp.arange(1, tapers + 1, dtype=jnp.int32).astype(jnp.float32)
    taper_rows = math.sqrt(2.0 / (length + 1)) * jnp.sin(math.pi * orders[:, None] * (frame_ids[None, :].astype(jnp.float32) + 1.0) / (length + 1))
    real_part = taper_rows[:, None, :] * jnp.cos(phase)[None]
    imag_part = -taper_rows[:, None, :] * jnp.sin(phase)[None]
    dft_table = jnp.stack([real_part, imag_part], axis=1)
    return dft_table.reshape(tapers * 2 * bins, length).astype(jnp.bfloat16)

def bin_cross(spectra, tapers, bins):
    rows_by_part = spectra.reshape(2 * tapers, bins, -1)
    per_bin = jnp.einsum('afp,bfp->fab', rows_by_part, rows_by_part, precision=lax.Precision.HIGHEST)
    return per_bin.reshape(bins, 4 * tapers * tapers)

def band_matrix(band_edges, bins):
    bin_ids = jnp.arange(bins, dtype=jnp.int32)
    band_mask = (bin_ids[None, :] >= band_edges[:-1, None]) & (bin_ids[None, :] < band_edges[1:, None])
    return band_mask.astype(jnp.float32)

def coherence_of(band_sums, counts, total_pixels, tapers):
    blocks = band_sums.reshape(-1, tapers, 2, tapers, 2)
    real_part = blocks[:, :, 0, :, 0] + blocks[:, :, 1, :, 1]
    imag_part = blocks[:, :, 1, :, 0] - blocks[:, :, 0, :, 1]
    power_diag = jnp.diagonal(real_part, axis1=1, axis2=2) + 1e-06
    denominator = jnp.sqrt(power_diag[:, :, None] * power_diag[:, None, :])
    scaling = jnp.sqrt(counts * jnp.float32(total_pixels))[:, None, None]
    off_diagonal = 1.0 - jnp.eye(tapers, dtype=jnp.float32)
    factor = scaling * off_diagonal / denominator
    return jnp.stack([real_part * factor, imag_part * factor], axis=1)

def centered_spectra(pixel_block, dft_table):
    widened = pixel_block.astype(jnp.float32)
    frame_mean = lax.optimization_barrier(jnp.mean(widened, axis=0, keepdims=True))
    centered = (widened - frame_mean).astype(jnp.bfloat16)
    return jnp.dot(dft_table.astype(jnp.float32), centered.astype(jnp.float32))

def reference(frames, band_edges):
    dft_table = transform_table(NT, NB, TAPERS)
    pixel_blocks = frames.reshape(NT, N_PIX * 8, PIX_DEV // 8).transpose(1, 0, 2)

    def accumulate(running, pixel_block):
        spectra = centered_spectra(pixel_block, dft_table)
        return (running + bin_cross(spectra, TAPERS, NB), None)
    running, _ = lax.scan(accumulate, jnp.zeros((NB, 4 * TAPERS * TAPERS), jnp.float32), pixel_blocks)
    band_mask = band_matrix(band_edges, NB)
    band_sums = jnp.dot(band_mask, running, precision=lax.Precision.HIGHEST)
    counts = lax.optimization_barrier(jnp.sum(band_mask, axis=1))
    return coherence_of(band_sums, counts, PIXELS, TAPERS)
```

```python
import functools
import math

import jax
import jax.numpy as jnp
from jax import lax
from jax.experimental import pallas as pl
from jax.experimental.pallas import tpu as pltpu
from jax.sharding import PartitionSpec as P

TAPERS = 8
NB = 384
NBANDS = 64
NT = 1024
CHUNK = 16
ROWS = CHUNK * TAPERS
LANES = 128
STEPS = NB // CHUNK
PIECE = 4
SLOTS = 2


FINE_COS, FINE_SIN, COARSE_COS, COARSE_SIN, TAPER = 0, CHUNK, 2 * CHUNK, 2 * CHUNK + STEPS, 2 * (CHUNK + STEPS)
WAVES = TAPER + TAPERS


def wave_kernel(waves_ref):
    def waves(count, stride):
        frame = lax.broadcasted_iota(jnp.int32, (count, NT), 1)
        bins = lax.broadcasted_iota(jnp.int32, (count, NT), 0) * stride
        phase = jnp.bitwise_and(bins * frame, NT - 1).astype(jnp.float32) * (2.0 * math.pi / NT)
        return jnp.cos(phase), jnp.sin(phase)

    cosine, sine = waves(CHUNK, 1)
    waves_ref[pl.ds(FINE_COS, CHUNK), :] = cosine
    waves_ref[pl.ds(FINE_SIN, CHUNK), :] = sine
    cosine, sine = waves(STEPS, CHUNK)
    waves_ref[pl.ds(COARSE_COS, STEPS), :] = cosine
    waves_ref[pl.ds(COARSE_SIN, STEPS), :] = sine
    order = lax.broadcasted_iota(jnp.int32, (TAPERS, NT), 0) + 1
    frame = lax.broadcasted_iota(jnp.int32, (TAPERS, NT), 1) + 1
    angle = (order * frame).astype(jnp.float32) * (math.pi / (NT + 1))
    waves_ref[pl.ds(TAPER, TAPERS), :] = math.sqrt(2.0 / (NT + 1)) * jnp.sin(angle)


def base_waves():
    return pl.pallas_call(
        wave_kernel,
        out_shape=jax.ShapeDtypeStruct((WAVES, NT), jnp.float32),
        cost_estimate=pl.CostEstimate(flops=10_000_000, bytes_accessed=400_000, transcendentals=100_000),
        name="base_waves",
    )()


def spectra_kernel(
    band_ref, keep_ref, waves_ref, data_ref, out_ref, table_ref, wave_ref, centered_ref, spectra_ref, band_sum_ref
):
    pixels = data_ref.shape[1]
    piece_rows = PIECE * 2 * ROWS
    pieces = STEPS // PIECE

    def table(p):
        taper = waves_ref[pl.ds(TAPER, TAPERS), :]
        for j in range(PIECE):
            a = p * PIECE + j
            ca, sa = waves_ref[pl.ds(COARSE_COS + a, 1), :], waves_ref[pl.ds(COARSE_SIN + a, 1), :]
            cb, sb = waves_ref[pl.ds(FINE_COS, CHUNK), :], waves_ref[pl.ds(FINE_SIN, CHUNK), :]
            wave_ref[a % 2, 0] = ca * cb - sa * sb
            wave_ref[a % 2, 1] = -(sa * cb + ca * sb)
            for part in range(2):
                for i in range(0, CHUNK, 2):
                    two = [taper * wave_ref[a % 2, part, pl.ds(i + h, 1), :] for h in range(2)]
                    at = j * 2 * ROWS + part * ROWS + i * TAPERS
                    table_ref[p % SLOTS, pl.ds(at, 2 * TAPERS), :] = jnp.concatenate(two, axis=0).astype(jnp.bfloat16)

    table(0)
    total = jnp.zeros((1, pixels), jnp.float32)
    for g in range(4):
        part = data_ref[pl.ds(g * 256, 256), :].astype(jnp.float32)
        total = total + jnp.sum(part, axis=0, keepdims=True)
    mean = total * (1.0 / NT)
    for g in range(4):
        part = data_ref[pl.ds(g * 256, 256), :].astype(jnp.float32)
        centered_ref[pl.ds(g * 256, 256), :] = (part - mean).astype(jnp.bfloat16)

    lane = lax.broadcasted_iota(jnp.int32, (TAPERS, LANES), 1)
    row = lax.broadcasted_iota(jnp.int32, (TAPERS, LANES), 0)
    is_real = lane < TAPERS

    def transform(p):
        spectra_ref[p % SLOTS] = jnp.dot(
            table_ref[p % SLOTS], centered_ref[...], preferred_element_type=jnp.float32
        ).astype(jnp.bfloat16)

    def cross(p, acc):
        for j in range(PIECE):
            both = spectra_ref[p % SLOTS, pl.ds(j * 2 * ROWS, 2 * ROWS), :]
            gram = lax.dot_general(both, both, (((1,), (1,)), ((), ())), preferred_element_type=jnp.float32)
            for i in range(CHUNK):
                f = (p * PIECE + j) * CHUNK + i
                top, low = i * TAPERS, ROWS + i * TAPERS
                real = gram[top : top + TAPERS, :LANES] + gram[low : low + TAPERS, LANES:]
                imag = gram[low : low + TAPERS, :LANES] - gram[top : top + TAPERS, LANES:]
                real = pltpu.roll(real, (LANES - top) % LANES, 1)
                imag = pltpu.roll(imag, (LANES - top + TAPERS) % LANES, 1)
                acc = acc * keep_ref[f] + jnp.where(is_real, real, imag)
                band_sum_ref[band_ref[f]] = acc
        return acc

    acc = jnp.zeros((TAPERS, LANES), jnp.float32)
    for p in range(pieces):
        transform(p)
        if p + 1 < pieces:
            table(p + 1)
        if p:
            acc = cross(p - 1, acc)
    acc = cross(pieces - 1, acc)
    value = jnp.where((lane < 2 * TAPERS)[None], band_sum_ref[...], 0.0)
    for shift in (16, 32, 64):
        value = value + pltpu.roll(value, shift, 2)
    own = (jnp.right_shift(lane, 4) == row)[None]
    sums = jnp.sum(jnp.where(own, value, 0.0), axis=1, keepdims=True)
    out_ref[...] = jnp.broadcast_to(sums, out_ref.shape)


def band_sums_of(data, waves, band_of, keep, copies):
    pixels = data.shape[1]
    vmem, smem = pl.BlockSpec(memory_space=pltpu.VMEM), pl.BlockSpec(memory_space=pltpu.SMEM)
    macs = 2 * NB * TAPERS * NT * pixels + STEPS * (2 * ROWS) ** 2 * pixels
    return pl.pallas_call(
        spectra_kernel,
        out_shape=jax.ShapeDtypeStruct((NBANDS, copies, LANES), jnp.float32),
        in_specs=[smem, smem, vmem, vmem],
        out_specs=vmem,
        scratch_shapes=[
            pltpu.VMEM((SLOTS, PIECE * 2 * ROWS, NT), jnp.bfloat16),
            pltpu.VMEM((2, 2, CHUNK, NT), jnp.float32),
            pltpu.VMEM((NT, pixels), jnp.bfloat16),
            pltpu.VMEM((SLOTS, PIECE * 2 * ROWS, pixels), jnp.bfloat16),
            pltpu.VMEM((NBANDS, TAPERS, LANES), jnp.float32),
        ],
        cost_estimate=pl.CostEstimate(flops=2 * macs, bytes_accessed=2_000_000, transcendentals=0),
        compiler_params=pltpu.CompilerParams(vmem_limit_bytes=20 * 2**20),
        name="band_sums",
    )(band_of, keep, waves, data)


def coherence_kernel(total_pixels, edges_ref, parts_ref, out_ref):
    own = lax.axis_index("tm")
    count = jnp.full((TAPERS, LANES), edges_ref[own + 1] - edges_ref[own], jnp.int32).astype(jnp.float32)
    scale = jnp.sqrt(count * jnp.float32(total_pixels))
    total = jnp.sum(parts_ref[...], axis=0, keepdims=True)
    lane = lax.broadcasted_iota(jnp.int32, (TAPERS, LANES), 1)
    row = lax.broadcasted_iota(jnp.int32, (TAPERS, LANES), 0)
    value = jnp.where(jnp.right_shift(lane, 4) == row, jnp.broadcast_to(total, (TAPERS, LANES)), 0.0)
    for shift in (16, 32, 64):
        value = value + pltpu.roll(value, shift, 1)
    diag = jnp.where(jnp.bitwise_and(lane, TAPERS * 2 - 1) == row, value, 0.0)
    diag = jnp.where(lane < TAPERS, diag, 0.0)
    power_row = jnp.sum(diag, axis=1, keepdims=True) + 1e-06
    power_lane = jnp.sum(diag, axis=0, keepdims=True)
    power_lane = jnp.where(lane < TAPERS, power_lane, pltpu.roll(jnp.broadcast_to(power_lane, (TAPERS, LANES)), TAPERS, 1)) + 1e-06
    denominator = jnp.sqrt(power_row * power_lane)
    off = jnp.bitwise_and(lane, TAPERS - 1) != row
    result = jnp.where(off, value * scale / denominator, 0.0)
    out_ref[0, 0] = result[:, :TAPERS]
    out_ref[0, 1] = result[:, TAPERS : 2 * TAPERS]


def coherence_of(band_edges, parts, total_pixels):
    return pl.pallas_call(
        functools.partial(coherence_kernel, total_pixels),
        out_shape=jax.ShapeDtypeStruct((1, 2, TAPERS, TAPERS), jnp.float32),
        in_specs=[pl.BlockSpec(memory_space=pltpu.SMEM), pl.BlockSpec(memory_space=pltpu.VMEM)],
        name="coherence",
    )(band_edges, parts)


def local(frames, band_edges):
    groups = lax.axis_size("tm")
    n_pix = lax.axis_size("pix")
    frames_dev, pix_dev = frames.shape
    share = pix_dev // groups
    blocks = frames.reshape(frames_dev, groups, share).transpose(1, 0, 2)
    data = lax.all_to_all(blocks, "tm", 0, 0, tiled=True).reshape(NT, share)
    waves = base_waves()
    bin_ids = jnp.arange(NB, dtype=jnp.int32)
    band_of = jnp.sum((bin_ids[:, None] >= band_edges[None, 1:]).astype(jnp.int32), axis=1)
    keep = 1.0 - jnp.any(bin_ids[:, None] == band_edges[None, :-1], axis=1).astype(jnp.float32)
    sums = band_sums_of(data, waves, band_of, keep, n_pix)
    parts = lax.all_to_all(sums.reshape(groups * n_pix, 1, LANES), ("tm", "pix"), 0, 0, tiled=True)
    return coherence_of(band_edges, parts.reshape(groups * n_pix, LANES), pix_dev * n_pix)


def solution(mesh):
    return jax.shard_map(
        local,
        mesh=mesh,
        in_specs=(P("tm", "pix"), P()),
        out_specs=P("tm", None, None, None),
        check_vma=False,
    )
```

```python
import functools
import math

import jax
import jax.numpy as jnp
from jax import lax
from jax.experimental import pallas as pl
from jax.experimental.pallas import tpu as pltpu
from jax.sharding import PartitionSpec as P

TAPERS = 8
NB = 384
NBANDS = 64
NT = 1024
CHUNK = 16
ROWS = CHUNK * TAPERS
LANES = 128
STEPS = NB // CHUNK
HALF = NT // 2
SLOTS = 2
MIDDLE = NT // 4
FULL = ((0, 1, 2, 3), (4, 5, 6, 7))
PAIRED = ((8, 9), (10, 11), (12, 13), (14, 15))
PIECES = FULL + PAIRED
PIECE_ROWS = 8 * ROWS


def base_waves():
    column = jnp.arange(NT, dtype=jnp.int32)
    frame = jnp.where(column < HALF, 2 * column, 2 * (column - HALF) + 1)[None]

    def waves(count, stride):
        bins = (jnp.arange(count, dtype=jnp.int32) * stride)[:, None]
        phase = jnp.bitwise_and(bins * frame, NT - 1).astype(jnp.float32) * (2.0 * math.pi / NT)
        return jnp.cos(phase), jnp.sin(phase)

    order = jnp.arange(1, TAPERS + 1, dtype=jnp.int32)[:, None]
    angle = (order * (frame + 1)).astype(jnp.float32) * (math.pi / (NT + 1))
    return *waves(CHUNK, 1), *waves(STEPS, CHUNK), math.sqrt(2.0 / (NT + 1)) * jnp.sin(angle)


def spectra_kernel(
    band_ref, keep_ref, fine_cos, fine_sin, coarse_cos, coarse_sin, taper_ref, data_ref, out_ref,
    wide_ref, table_ref, wave_ref, centered_ref, spectra_ref, middle_ref, low_sum_ref, high_sum_ref,
):
    pixels = data_ref.shape[1]

    def wave(a, slot):
        ca, sa = coarse_cos[pl.ds(a, 1), :], coarse_sin[pl.ds(a, 1), :]
        cb, sb = fine_cos[...], fine_sin[...]
        wave_ref[slot, 0] = ca * cb - sa * sb
        wave_ref[slot, 1] = -(sa * cb + ca * sb)

    def table(p):
        taper = taper_ref[...]
        for j, a in enumerate(PIECES[p]):
            wave(a, a % 2)
            for part in range(2):
                for i in range(0, CHUNK, 2):
                    two = [taper * wave_ref[a % 2, part, pl.ds(i + h, 1), :] for h in range(2)]
                    at = j * 2 * ROWS + part * ROWS + i * TAPERS
                    table_ref[p % SLOTS, pl.ds(at, 2 * TAPERS), :] = jnp.concatenate(two, axis=0).astype(jnp.bfloat16)
        if p == len(FULL) - 1:
            wave(MIDDLE // CHUNK, 2)
            two = [taper * wave_ref[2, part, pl.ds(0, 1), :] for part in range(2)]
            table_ref[p % SLOTS, pl.ds(PIECE_ROWS, 2 * TAPERS), :] = jnp.concatenate(two, axis=0).astype(jnp.bfloat16)

    table(0)
    low_sum_ref[...] = jnp.zeros(low_sum_ref.shape, jnp.float32)
    high_sum_ref[...] = jnp.zeros(high_sum_ref.shape, jnp.float32)
    total = jnp.zeros((1, pixels), jnp.float32)
    for g in range(4):
        part = data_ref[pl.ds(g * 256, 256), :].astype(jnp.float32)
        total = total + jnp.sum(part, axis=0, keepdims=True)
        for h in range(pixels // LANES):
            wide_ref[h, pl.ds(g * 256, 256), :] = part[:, h * LANES : (h + 1) * LANES]
    mean = total * (1.0 / NT)
    for odd in range(2):
        for h in range(pixels // LANES):
            part = wide_ref[h, pl.ds(odd, HALF, stride=2), :] - mean[:, h * LANES : (h + 1) * LANES]
            centered_ref[pl.ds(odd * HALF, HALF), h * LANES : (h + 1) * LANES] = part.astype(jnp.bfloat16)

    lane = lax.broadcasted_iota(jnp.int32, (TAPERS, LANES), 1)
    row = lax.broadcasted_iota(jnp.int32, (TAPERS, LANES), 0)
    is_real = lane < TAPERS

    def transform(p):
        slot = p % SLOTS
        if p < len(FULL):
            rows = PIECE_ROWS + (2 * TAPERS if p == len(FULL) - 1 else 0)
            value = jnp.dot(table_ref[slot, pl.ds(0, rows), :], centered_ref[...], preferred_element_type=jnp.float32)
            spectra_ref[slot] = value[:PIECE_ROWS].astype(jnp.bfloat16)
            if rows > PIECE_ROWS:
                middle_ref[...] = value[PIECE_ROWS:]
            return
        rows = PIECE_ROWS // 2
        even = jnp.dot(
            table_ref[slot, pl.ds(0, rows), pl.ds(0, HALF)], centered_ref[pl.ds(0, HALF), :], preferred_element_type=jnp.float32
        )
        odd = jnp.dot(
            table_ref[slot, pl.ds(0, rows), pl.ds(HALF, HALF)], centered_ref[pl.ds(HALF, HALF), :], preferred_element_type=jnp.float32
        )
        spectra_ref[slot, pl.ds(0, rows), :] = (even + odd).astype(jnp.bfloat16)
        mirror = even - odd
        if p == len(FULL):
            mirror = jnp.concatenate(
                [
                    middle_ref[pl.ds(0, TAPERS), :],
                    mirror[TAPERS:ROWS],
                    -middle_ref[pl.ds(TAPERS, TAPERS), :],
                    mirror[ROWS + TAPERS :],
                ],
                axis=0,
            )
        spectra_ref[slot, pl.ds(rows, rows), :] = mirror.astype(jnp.bfloat16)

    def values(p, j, mirrored):
        both = spectra_ref[p % SLOTS, pl.ds(j * 2 * ROWS, 2 * ROWS), :]
        gram = lax.dot_general(both, both, (((1,), (1,)), ((), ())), preferred_element_type=jnp.float32)
        found = []
        for i in range(CHUNK):
            top, low = i * TAPERS, ROWS + i * TAPERS
            real = gram[top : top + TAPERS, :LANES] + gram[low : low + TAPERS, LANES:]
            imag = gram[low : low + TAPERS, :LANES] - gram[top : top + TAPERS, LANES:]
            if mirrored:
                imag = -imag
            real = pltpu.roll(real, (LANES - top) % LANES, 1)
            imag = pltpu.roll(imag, (LANES - top + TAPERS) % LANES, 1)
            found.append(jnp.where(is_real, real, imag))
        return found

    zero = jnp.zeros((TAPERS, LANES), jnp.float32)
    state = {"low": zero, "high": zero, "middle": zero}

    def add_high(f, value):
        state["high"] = state["high"] * keep_ref[f + 1] + value
        high_sum_ref[band_ref[f]] = state["high"]

    def cross(p):
        for j, a in enumerate(PIECES[p]):
            for i, value in enumerate(values(p, j, False)):
                f = a * CHUNK + i
                state["low"] = state["low"] * keep_ref[f] + value
                low_sum_ref[band_ref[f]] = state["low"]
        if p < len(FULL):
            return
        for j, a in enumerate(PIECES[p]):
            for i, value in enumerate(values(p, len(PIECES[p]) + j, True)):
                f = HALF - (a * CHUNK + i)
                if f == NB:
                    state["middle"] = value
                else:
                    add_high(f, value)

    for p in range(len(PIECES)):
        transform(p)
        if p + 1 < len(PIECES):
            table(p + 1)
        if p:
            cross(p - 1)
    cross(len(PIECES) - 1)
    add_high(MIDDLE, state["middle"])
    value = jnp.where((lane < 2 * TAPERS)[None], low_sum_ref[...] + high_sum_ref[...], 0.0)
    for shift in (16, 32, 64):
        value = value + pltpu.roll(value, shift, 2)
    own = (jnp.right_shift(lane, 4) == row)[None]
    sums = jnp.sum(jnp.where(own, value, 0.0), axis=1, keepdims=True)
    out_ref[...] = jnp.broadcast_to(sums, out_ref.shape)


def band_sums_of(data, waves, band_of, keep, copies):
    pixels = data.shape[1]
    vmem, smem = pl.BlockSpec(memory_space=pltpu.VMEM), pl.BlockSpec(memory_space=pltpu.SMEM)
    macs = NB * TAPERS * NT * pixels * 4 // 3 + STEPS * (2 * ROWS) ** 2 * pixels
    return pl.pallas_call(
        spectra_kernel,
        out_shape=jax.ShapeDtypeStruct((NBANDS, copies, LANES), jnp.float32),
        in_specs=[smem, smem] + [vmem] * 6,
        out_specs=vmem,
        scratch_shapes=[
            pltpu.VMEM((pixels // LANES, NT, LANES), jnp.float32),
            pltpu.VMEM((SLOTS, PIECE_ROWS + 2 * TAPERS, NT), jnp.bfloat16),
            pltpu.VMEM((3, 2, CHUNK, NT), jnp.float32),
            pltpu.VMEM((NT, pixels), jnp.bfloat16),
            pltpu.VMEM((SLOTS, PIECE_ROWS, pixels), jnp.bfloat16),
            pltpu.VMEM((2 * TAPERS, pixels), jnp.float32),
            pltpu.VMEM((NBANDS, TAPERS, LANES), jnp.float32),
            pltpu.VMEM((NBANDS, TAPERS, LANES), jnp.float32),
        ],
        cost_estimate=pl.CostEstimate(flops=2 * macs, bytes_accessed=2_000_000, transcendentals=0),
        compiler_params=pltpu.CompilerParams(vmem_limit_bytes=28 * 2**20),
        name="band_sums",
    )(band_of, keep, *waves, data)


def coherence_kernel(total_pixels, edges_ref, parts_ref, out_ref):
    own = lax.axis_index("tm")
    count = jnp.full((TAPERS, LANES), edges_ref[own + 1] - edges_ref[own], jnp.int32).astype(jnp.float32)
    scale = jnp.sqrt(count * jnp.float32(total_pixels))
    total = jnp.sum(parts_ref[...], axis=0, keepdims=True)
    lane = lax.broadcasted_iota(jnp.int32, (TAPERS, LANES), 1)
    row = lax.broadcasted_iota(jnp.int32, (TAPERS, LANES), 0)
    value = jnp.where(jnp.right_shift(lane, 4) == row, jnp.broadcast_to(total, (TAPERS, LANES)), 0.0)
    for shift in (16, 32, 64):
        value = value + pltpu.roll(value, shift, 1)
    diag = jnp.where(jnp.bitwise_and(lane, TAPERS * 2 - 1) == row, value, 0.0)
    diag = jnp.where(lane < TAPERS, diag, 0.0)
    power_row = jnp.sum(diag, axis=1, keepdims=True) + 1e-06
    power_lane = jnp.sum(diag, axis=0, keepdims=True)
    power_lane = jnp.where(lane < TAPERS, power_lane, pltpu.roll(jnp.broadcast_to(power_lane, (TAPERS, LANES)), TAPERS, 1)) + 1e-06
    denominator = jnp.sqrt(power_row * power_lane)
    off = jnp.bitwise_and(lane, TAPERS - 1) != row
    result = jnp.where(off, value * scale / denominator, 0.0)
    out_ref[0, 0] = result[:, :TAPERS]
    out_ref[0, 1] = result[:, TAPERS : 2 * TAPERS]


def coherence_of(band_edges, parts, total_pixels):
    return pl.pallas_call(
        functools.partial(coherence_kernel, total_pixels),
        out_shape=jax.ShapeDtypeStruct((1, 2, TAPERS, TAPERS), jnp.float32),
        in_specs=[pl.BlockSpec(memory_space=pltpu.SMEM), pl.BlockSpec(memory_space=pltpu.VMEM)],
        name="coherence",
    )(band_edges, parts)


def local(frames, band_edges):
    groups = lax.axis_size("tm")
    n_pix = lax.axis_size("pix")
    frames_dev, pix_dev = frames.shape
    share = pix_dev // groups
    blocks = frames.reshape(frames_dev, groups, share).transpose(1, 0, 2)
    data = lax.all_to_all(blocks, "tm", 0, 0, tiled=True).reshape(NT, share)
    waves = base_waves()
    bin_ids = jnp.arange(NB + 1, dtype=jnp.int32)
    band_of = jnp.sum((bin_ids[:, None] >= band_edges[None, 1:]).astype(jnp.int32), axis=1)
    keep = 1.0 - jnp.any(bin_ids[:, None] == band_edges[None, :], axis=1).astype(jnp.float32)
    sums = band_sums_of(data, waves, band_of, keep, n_pix)
    parts = lax.all_to_all(sums.reshape(groups * n_pix, 1, LANES), ("tm", "pix"), 0, 0, tiled=True)
    return coherence_of(band_edges, parts.reshape(groups * n_pix, LANES), pix_dev * n_pix)


def solution(mesh):
    return jax.shard_map(
        local,
        mesh=mesh,
        in_specs=(P("tm", "pix"), P()),
        out_specs=P("tm", None, None, None),
        check_vma=False,
    )
```

```python
import functools
import math

import jax
import jax.numpy as jnp
from jax import lax
from jax.experimental import pallas as pl
from jax.experimental.pallas import tpu as pltpu
from jax.sharding import PartitionSpec as P

TAPERS = 8
NB = 384
NBANDS = 64
NT = 1024
CHUNK = 16
ROWS = CHUNK * TAPERS
LANES = 128
STEPS = NB // CHUNK
HALF = NT // 2
SLOTS = 2
MIDDLE = NT // 4
FULL = ((0, 1, 2, 3), (4, 5, 6, 7))
PAIRED = ((8, 9), (10, 11), (12, 13), (14, 15))
PIECES = FULL + PAIRED
PIECE_ROWS = 8 * ROWS


def base_waves():
    column = jnp.arange(NT, dtype=jnp.int32)
    frame = jnp.where(column < HALF, 2 * column, 2 * (column - HALF) + 1)[None]

    def waves(count, stride):
        bins = (jnp.arange(count, dtype=jnp.int32) * stride)[:, None]
        phase = jnp.bitwise_and(bins * frame, NT - 1).astype(jnp.float32) * (2.0 * math.pi / NT)
        return jnp.cos(phase), jnp.sin(phase)

    order = jnp.arange(1, TAPERS + 1, dtype=jnp.int32)[:, None]
    angle = (order * (frame + 1)).astype(jnp.float32) * (math.pi / (NT + 1))
    return *waves(CHUNK, 1), *waves(STEPS, CHUNK), math.sqrt(2.0 / (NT + 1)) * jnp.sin(angle)


def spectra_kernel(
    band_ref, keep_ref, fine_cos, fine_sin, coarse_cos, coarse_sin, taper_ref, data_ref, out_ref,
    wide_ref, table_ref, wave_ref, centered_ref, spectra_ref, middle_ref, low_sum_ref, high_sum_ref,
):
    pixels = data_ref.shape[1]

    def wave(a, slot):
        ca, sa = coarse_cos[pl.ds(a, 1), :], coarse_sin[pl.ds(a, 1), :]
        cb, sb = fine_cos[...], fine_sin[...]
        wave_ref[slot, 0] = ca * cb - sa * sb
        wave_ref[slot, 1] = -(sa * cb + ca * sb)

    def table(p):
        taper = taper_ref[...]
        for j, a in enumerate(PIECES[p]):
            wave(a, a % 2)
            for part in range(2):
                for i in range(0, CHUNK, 2):
                    two = [taper * wave_ref[a % 2, part, pl.ds(i + h, 1), :] for h in range(2)]
                    at = j * 2 * ROWS + part * ROWS + i * TAPERS
                    table_ref[p % SLOTS, pl.ds(at, 2 * TAPERS), :] = jnp.concatenate(two, axis=0).astype(jnp.bfloat16)
        if p == len(FULL) - 1:
            wave(MIDDLE // CHUNK, 2)
            two = [taper * wave_ref[2, part, pl.ds(0, 1), :] for part in range(2)]
            table_ref[p % SLOTS, pl.ds(PIECE_ROWS, 2 * TAPERS), :] = jnp.concatenate(two, axis=0).astype(jnp.bfloat16)

    table(0)
    low_sum_ref[...] = jnp.zeros(low_sum_ref.shape, jnp.float32)
    high_sum_ref[...] = jnp.zeros(high_sum_ref.shape, jnp.float32)
    total = jnp.zeros((1, pixels), jnp.float32)
    for g in range(4):
        part = data_ref[pl.ds(g * 256, 256), :].astype(jnp.float32)
        total = total + jnp.sum(part, axis=0, keepdims=True)
        for h in range(pixels // LANES):
            wide_ref[h, pl.ds(g * 256, 256), :] = part[:, h * LANES : (h + 1) * LANES]
    mean = total * (1.0 / NT)
    for odd in range(2):
        for h in range(pixels // LANES):
            part = wide_ref[h, pl.ds(odd, HALF, stride=2), :] - mean[:, h * LANES : (h + 1) * LANES]
            centered_ref[pl.ds(odd * HALF, HALF), h * LANES : (h + 1) * LANES] = part.astype(jnp.bfloat16)

    lane = lax.broadcasted_iota(jnp.int32, (TAPERS, LANES), 1)
    row = lax.broadcasted_iota(jnp.int32, (TAPERS, LANES), 0)
    is_real = lane < TAPERS

    def transform(p):
        slot = p % SLOTS
        if p < len(FULL):
            rows = PIECE_ROWS + (2 * TAPERS if p == len(FULL) - 1 else 0)
            value = jnp.dot(table_ref[slot, pl.ds(0, rows), :], centered_ref[...], preferred_element_type=jnp.float32)
            spectra_ref[slot] = value[:PIECE_ROWS].astype(jnp.bfloat16)
            if rows > PIECE_ROWS:
                middle_ref[...] = value[PIECE_ROWS:]
            return
        rows = PIECE_ROWS // 2
        even = jnp.dot(
            table_ref[slot, pl.ds(0, rows), pl.ds(0, HALF)], centered_ref[pl.ds(0, HALF), :], preferred_element_type=jnp.float32
        )
        odd = jnp.dot(
            table_ref[slot, pl.ds(0, rows), pl.ds(HALF, HALF)], centered_ref[pl.ds(HALF, HALF), :], preferred_element_type=jnp.float32
        )
        spectra_ref[slot, pl.ds(0, rows), :] = (even + odd).astype(jnp.bfloat16)
        mirror = even - odd
        if p == len(FULL):
            mirror = jnp.concatenate(
                [
                    middle_ref[pl.ds(0, TAPERS), :],
                    mirror[TAPERS:ROWS],
                    -middle_ref[pl.ds(TAPERS, TAPERS), :],
                    mirror[ROWS + TAPERS :],
                ],
                axis=0,
            )
        spectra_ref[slot, pl.ds(rows, rows), :] = mirror.astype(jnp.bfloat16)

    def values(p, j, mirrored):
        both = spectra_ref[p % SLOTS, pl.ds(j * 2 * ROWS, 2 * ROWS), :]
        gram = lax.dot_general(both, both, (((1,), (1,)), ((), ())), preferred_element_type=jnp.float32)
        found = []
        for i in range(CHUNK):
            top, low = i * TAPERS, ROWS + i * TAPERS
            real = gram[top : top + TAPERS, :LANES] + gram[low : low + TAPERS, LANES:]
            imag = gram[low : low + TAPERS, :LANES] - gram[top : top + TAPERS, LANES:]
            if mirrored:
                imag = -imag
            real = pltpu.roll(real, (LANES - top) % LANES, 1)
            imag = pltpu.roll(imag, (LANES - top + TAPERS) % LANES, 1)
            found.append(jnp.where(is_real, real, imag))
        return found

    zero = jnp.zeros((TAPERS, LANES), jnp.float32)
    state = {"low": zero, "high": zero, "middle": zero}

    def add_high(f, value):
        state["high"] = state["high"] * keep_ref[f + 1] + value
        high_sum_ref[band_ref[f]] = state["high"]

    def cross(p):
        for j, a in enumerate(PIECES[p]):
            for i, value in enumerate(values(p, j, False)):
                f = a * CHUNK + i
                state["low"] = state["low"] * keep_ref[f] + value
                low_sum_ref[band_ref[f]] = state["low"]
        if p < len(FULL):
            return
        for j, a in enumerate(PIECES[p]):
            for i, value in enumerate(values(p, len(PIECES[p]) + j, True)):
                f = HALF - (a * CHUNK + i)
                if f == NB:
                    state["middle"] = value
                else:
                    add_high(f, value)

    for p in range(len(PIECES)):
        transform(p)
        if p + 1 < len(PIECES):
            table(p + 1)
        if p:
            cross(p - 1)
    cross(len(PIECES) - 1)
    add_high(MIDDLE, state["middle"])
    value = jnp.where((lane < 2 * TAPERS)[None], low_sum_ref[...] + high_sum_ref[...], 0.0)
    for shift in (16, 32, 64):
        value = value + pltpu.roll(value, shift, 2)
    own = (jnp.right_shift(lane, 4) == row)[None]
    sums = jnp.sum(jnp.where(own, value, 0.0), axis=1, keepdims=True)
    out_ref[...] = jnp.broadcast_to(sums, out_ref.shape)


def band_sums_of(data, waves, band_of, keep, copies):
    pixels = data.shape[1]
    vmem, smem = pl.BlockSpec(memory_space=pltpu.VMEM), pl.BlockSpec(memory_space=pltpu.SMEM)
    macs = NB * TAPERS * NT * pixels * 4 // 3 + STEPS * (2 * ROWS) ** 2 * pixels
    return pl.pallas_call(
        spectra_kernel,
        out_shape=jax.ShapeDtypeStruct((NBANDS, copies, LANES), jnp.float32),
        in_specs=[smem, smem] + [vmem] * 6,
        out_specs=vmem,
        scratch_shapes=[
            pltpu.VMEM((pixels // LANES, NT, LANES), jnp.float32),
            pltpu.VMEM((SLOTS, PIECE_ROWS + 2 * TAPERS, NT), jnp.bfloat16),
            pltpu.VMEM((3, 2, CHUNK, NT), jnp.float32),
            pltpu.VMEM((NT, pixels), jnp.bfloat16),
            pltpu.VMEM((SLOTS, PIECE_ROWS, pixels), jnp.bfloat16),
            pltpu.VMEM((2 * TAPERS, pixels), jnp.float32),
            pltpu.VMEM((NBANDS, TAPERS, LANES), jnp.float32),
            pltpu.VMEM((NBANDS, TAPERS, LANES), jnp.float32),
        ],
        cost_estimate=pl.CostEstimate(flops=2 * macs, bytes_accessed=2_000_000, transcendentals=0),
        compiler_params=pltpu.CompilerParams(vmem_limit_bytes=28 * 2**20),
        name="band_sums",
    )(band_of, keep, *waves, data)


def split_kernel(frames_ref, blocks_ref, sem):
    groups, _, share = blocks_ref.shape
    for j in range(groups):
        pltpu.make_async_copy(frames_ref.at[:, pl.ds(j * share, share)], blocks_ref.at[j], sem).start()
    pltpu.make_async_copy(blocks_ref, blocks_ref, sem).wait()


def split_pixels(frames, groups):
    rows, pixels = frames.shape
    return pl.pallas_call(
        split_kernel,
        out_shape=jax.ShapeDtypeStruct((groups, rows, pixels // groups), frames.dtype),
        in_specs=[pl.BlockSpec(memory_space=pl.ANY)],
        out_specs=pl.BlockSpec(memory_space=pltpu.VMEM),
        scratch_shapes=[pltpu.SemaphoreType.DMA],
        name="split_pixels",
    )(frames)


def coherence_kernel(total_pixels, edges_ref, parts_ref, out_ref):
    own = lax.axis_index("tm")
    count = jnp.full((TAPERS, LANES), edges_ref[own + 1] - edges_ref[own], jnp.int32).astype(jnp.float32)
    scale = jnp.sqrt(count * jnp.float32(total_pixels))
    total = jnp.sum(parts_ref[...], axis=0, keepdims=True)
    lane = lax.broadcasted_iota(jnp.int32, (TAPERS, LANES), 1)
    row = lax.broadcasted_iota(jnp.int32, (TAPERS, LANES), 0)
    value = jnp.where(jnp.right_shift(lane, 4) == row, jnp.broadcast_to(total, (TAPERS, LANES)), 0.0)
    for shift in (16, 32, 64):
        value = value + pltpu.roll(value, shift, 1)
    diag = jnp.where(jnp.bitwise_and(lane, TAPERS * 2 - 1) == row, value, 0.0)
    diag = jnp.where(lane < TAPERS, diag, 0.0)
    power_row = jnp.sum(diag, axis=1, keepdims=True) + 1e-06
    power_lane = jnp.sum(diag, axis=0, keepdims=True)
    power_lane = jnp.where(lane < TAPERS, power_lane, pltpu.roll(jnp.broadcast_to(power_lane, (TAPERS, LANES)), TAPERS, 1)) + 1e-06
    denominator = jnp.sqrt(power_row * power_lane)
    off = jnp.bitwise_and(lane, TAPERS - 1) != row
    result = jnp.where(off, value * scale / denominator, 0.0)
    out_ref[0, 0] = result[:, :TAPERS]
    out_ref[0, 1] = result[:, TAPERS : 2 * TAPERS]


def coherence_of(band_edges, parts, total_pixels):
    return pl.pallas_call(
        functools.partial(coherence_kernel, total_pixels),
        out_shape=jax.ShapeDtypeStruct((1, 2, TAPERS, TAPERS), jnp.float32),
        in_specs=[pl.BlockSpec(memory_space=pltpu.SMEM), pl.BlockSpec(memory_space=pltpu.VMEM)],
        name="coherence",
    )(band_edges, parts)


def local(frames, band_edges):
    groups = lax.axis_size("tm")
    n_pix = lax.axis_size("pix")
    pix_dev = frames.shape[1]
    share = pix_dev // groups
    blocks = split_pixels(frames, groups)
    data = lax.all_to_all(blocks, "tm", 0, 0, tiled=True).reshape(NT, share)
    waves = base_waves()
    bin_ids = jnp.arange(NB + 1, dtype=jnp.int32)
    band_of = jnp.sum((bin_ids[:, None] >= band_edges[None, 1:]).astype(jnp.int32), axis=1)
    keep = 1.0 - jnp.any(bin_ids[:, None] == band_edges[None, :], axis=1).astype(jnp.float32)
    sums = band_sums_of(data, waves, band_of, keep, n_pix)
    parts = lax.all_to_all(sums.reshape(groups * n_pix, 1, LANES), ("tm", "pix"), 0, 0, tiled=True)
    return coherence_of(band_edges, parts.reshape(groups * n_pix, LANES), pix_dev * n_pix)


def solution(mesh):
    return jax.shard_map(
        local,
        mesh=mesh,
        in_specs=(P("tm", "pix"), P()),
        out_specs=P("tm", None, None, None),
        check_vma=False,
    )
```

```python
import functools
import math

import jax
import jax.numpy as jnp
from jax import lax
from jax.experimental import pallas as pl
from jax.experimental.pallas import tpu as pltpu
from jax.sharding import PartitionSpec as P

TAPERS = 8
NB = 384
NBANDS = 64
NT = 1024
CHUNK = 16
ROWS = CHUNK * TAPERS
LANES = 128
STEPS = NB // CHUNK
HALF = NT // 2
SLOTS = 2
MIDDLE = NT // 4
FULL = ((0, 1, 2, 3), (4, 5, 6, 7))
PAIRED = ((8, 9), (10, 11), (12, 13), (14, 15))
PIECES = FULL + PAIRED
PIECE_ROWS = 8 * ROWS


def base_waves():
    column = jnp.arange(NT, dtype=jnp.int32)
    frame = jnp.where(column < HALF, 2 * column, 2 * (column - HALF) + 1)[None]

    def waves(count, stride):
        bins = (jnp.arange(count, dtype=jnp.int32) * stride)[:, None]
        phase = jnp.bitwise_and(bins * frame, NT - 1).astype(jnp.float32) * (2.0 * math.pi / NT)
        return jnp.cos(phase), jnp.sin(phase)

    order = jnp.arange(1, TAPERS + 1, dtype=jnp.int32)[:, None]
    angle = (order * (frame + 1)).astype(jnp.float32) * (math.pi / (NT + 1))
    return *waves(CHUNK, 1), *waves(STEPS, CHUNK), math.sqrt(2.0 / (NT + 1)) * jnp.sin(angle)


def spectra_kernel(
    band_ref, keep_ref, fine_cos, fine_sin, coarse_cos, coarse_sin, taper_ref, data_ref, out_ref,
    wide_ref, table_ref, wave_ref, centered_ref, spectra_ref, middle_ref, low_sum_ref, high_sum_ref,
):
    pixels = data_ref.shape[1]

    def wave(a, slot):
        ca, sa = coarse_cos[pl.ds(a, 1), :], coarse_sin[pl.ds(a, 1), :]
        cb, sb = fine_cos[...], fine_sin[...]
        wave_ref[slot, 0] = ca * cb - sa * sb
        wave_ref[slot, 1] = -(sa * cb + ca * sb)

    def table(p):
        taper = taper_ref[...]
        for j, a in enumerate(PIECES[p]):
            wave(a, a % 2)
            for part in range(2):
                for i in range(0, CHUNK, 2):
                    two = [taper * wave_ref[a % 2, part, pl.ds(i + h, 1), :] for h in range(2)]
                    at = j * 2 * ROWS + part * ROWS + i * TAPERS
                    table_ref[p % SLOTS, pl.ds(at, 2 * TAPERS), :] = jnp.concatenate(two, axis=0).astype(jnp.bfloat16)
        if p == len(FULL) - 1:
            wave(MIDDLE // CHUNK, 2)
            two = [taper * wave_ref[2, part, pl.ds(0, 1), :] for part in range(2)]
            table_ref[p % SLOTS, pl.ds(PIECE_ROWS, 2 * TAPERS), :] = jnp.concatenate(two, axis=0).astype(jnp.bfloat16)

    table(0)
    low_sum_ref[...] = jnp.zeros(low_sum_ref.shape, jnp.float32)
    high_sum_ref[...] = jnp.zeros(high_sum_ref.shape, jnp.float32)
    total = jnp.zeros((1, pixels), jnp.float32)
    for g in range(4):
        part = data_ref[pl.ds(g * 256, 256), :].astype(jnp.float32)
        total = total + jnp.sum(part, axis=0, keepdims=True)
        for h in range(pixels // LANES):
            wide_ref[h, pl.ds(g * 256, 256), :] = part[:, h * LANES : (h + 1) * LANES]
    mean = total * (1.0 / NT)
    for odd in range(2):
        for h in range(pixels // LANES):
            part = wide_ref[h, pl.ds(odd, HALF, stride=2), :] - mean[:, h * LANES : (h + 1) * LANES]
            centered_ref[pl.ds(odd * HALF, HALF), h * LANES : (h + 1) * LANES] = part.astype(jnp.bfloat16)

    lane = lax.broadcasted_iota(jnp.int32, (TAPERS, LANES), 1)
    row = lax.broadcasted_iota(jnp.int32, (TAPERS, LANES), 0)
    is_real = lane < TAPERS

    def transform(p):
        slot = p % SLOTS
        if p < len(FULL):
            rows = PIECE_ROWS + (2 * TAPERS if p == len(FULL) - 1 else 0)
            value = jnp.dot(table_ref[slot, pl.ds(0, rows), :], centered_ref[...], preferred_element_type=jnp.float32)
            spectra_ref[slot] = value[:PIECE_ROWS].astype(jnp.bfloat16)
            if rows > PIECE_ROWS:
                middle_ref[...] = value[PIECE_ROWS:]
            return
        rows = PIECE_ROWS // 2
        even = jnp.dot(
            table_ref[slot, pl.ds(0, rows), pl.ds(0, HALF)], centered_ref[pl.ds(0, HALF), :], preferred_element_type=jnp.float32
        )
        odd = jnp.dot(
            table_ref[slot, pl.ds(0, rows), pl.ds(HALF, HALF)], centered_ref[pl.ds(HALF, HALF), :], preferred_element_type=jnp.float32
        )
        spectra_ref[slot, pl.ds(0, rows), :] = (even + odd).astype(jnp.bfloat16)
        mirror = even - odd
        if p == len(FULL):
            mirror = jnp.concatenate(
                [
                    middle_ref[pl.ds(0, TAPERS), :],
                    mirror[TAPERS:ROWS],
                    -middle_ref[pl.ds(TAPERS, TAPERS), :],
                    mirror[ROWS + TAPERS :],
                ],
                axis=0,
            )
        spectra_ref[slot, pl.ds(rows, rows), :] = mirror.astype(jnp.bfloat16)

    def values(p, j, mirrored):
        both = spectra_ref[p % SLOTS, pl.ds(j * 2 * ROWS, 2 * ROWS), :]
        gram = lax.dot_general(both, both, (((1,), (1,)), ((), ())), preferred_element_type=jnp.float32)
        found = []
        for i in range(CHUNK):
            top, low = i * TAPERS, ROWS + i * TAPERS
            real = gram[top : top + TAPERS, :LANES] + gram[low : low + TAPERS, LANES:]
            imag = gram[low : low + TAPERS, :LANES] - gram[top : top + TAPERS, LANES:]
            if mirrored:
                imag = -imag
            real = pltpu.roll(real, (LANES - top) % LANES, 1)
            imag = pltpu.roll(imag, (LANES - top + TAPERS) % LANES, 1)
            found.append(jnp.where(is_real, real, imag))
        return found

    zero = jnp.zeros((TAPERS, LANES), jnp.float32)
    state = {"low": zero, "high": zero, "middle": zero}

    def add_high(f, value):
        state["high"] = state["high"] * keep_ref[f + 1] + value
        high_sum_ref[band_ref[f]] = state["high"]

    def cross(p):
        for j, a in enumerate(PIECES[p]):
            for i, value in enumerate(values(p, j, False)):
                f = a * CHUNK + i
                state["low"] = state["low"] * keep_ref[f] + value
                low_sum_ref[band_ref[f]] = state["low"]
        if p < len(FULL):
            return
        for j, a in enumerate(PIECES[p]):
            for i, value in enumerate(values(p, len(PIECES[p]) + j, True)):
                f = HALF - (a * CHUNK + i)
                if f == NB:
                    state["middle"] = value
                else:
                    add_high(f, value)

    for p in range(len(PIECES)):
        transform(p)
        if p + 1 < len(PIECES):
            table(p + 1)
        if p:
            cross(p - 1)
    cross(len(PIECES) - 1)
    add_high(MIDDLE, state["middle"])
    value = jnp.where((lane < 2 * TAPERS)[None], low_sum_ref[...] + high_sum_ref[...], 0.0)
    for shift in (16, 32, 64):
        value = value + pltpu.roll(value, shift, 2)
    own = (jnp.right_shift(lane, 4) == row)[None]
    sums = jnp.sum(jnp.where(own, value, 0.0), axis=1)
    for i in range(out_ref.shape[0]):
        out_ref[i] = sums


def band_sums_of(data, waves, band_of, keep, copies):
    pixels = data.shape[1]
    vmem, smem = pl.BlockSpec(memory_space=pltpu.VMEM), pl.BlockSpec(memory_space=pltpu.SMEM)
    macs = NB * TAPERS * NT * pixels * 4 // 3 + STEPS * (2 * ROWS) ** 2 * pixels
    return pl.pallas_call(
        spectra_kernel,
        out_shape=jax.ShapeDtypeStruct((copies, NBANDS, LANES), jnp.float32),
        in_specs=[smem, smem] + [vmem] * 6,
        out_specs=vmem,
        scratch_shapes=[
            pltpu.VMEM((pixels // LANES, NT, LANES), jnp.float32),
            pltpu.VMEM((SLOTS, PIECE_ROWS + 2 * TAPERS, NT), jnp.bfloat16),
            pltpu.VMEM((3, 2, CHUNK, NT), jnp.float32),
            pltpu.VMEM((NT, pixels), jnp.bfloat16),
            pltpu.VMEM((SLOTS, PIECE_ROWS, pixels), jnp.bfloat16),
            pltpu.VMEM((2 * TAPERS, pixels), jnp.float32),
            pltpu.VMEM((NBANDS, TAPERS, LANES), jnp.float32),
            pltpu.VMEM((NBANDS, TAPERS, LANES), jnp.float32),
        ],
        cost_estimate=pl.CostEstimate(flops=2 * macs, bytes_accessed=2_000_000, transcendentals=0),
        compiler_params=pltpu.CompilerParams(vmem_limit_bytes=28 * 2**20),
        name="band_sums",
    )(band_of, keep, *waves, data)


def split_kernel(frames_ref, blocks_ref, sem):
    groups, _, share = blocks_ref.shape
    for j in range(groups):
        pltpu.make_async_copy(frames_ref.at[:, pl.ds(j * share, share)], blocks_ref.at[j], sem).start()
    pltpu.make_async_copy(blocks_ref, blocks_ref, sem).wait()


def split_pixels(frames, groups):
    rows, pixels = frames.shape
    return pl.pallas_call(
        split_kernel,
        out_shape=jax.ShapeDtypeStruct((groups, rows, pixels // groups), frames.dtype),
        in_specs=[pl.BlockSpec(memory_space=pl.ANY)],
        out_specs=pl.BlockSpec(memory_space=pltpu.VMEM),
        scratch_shapes=[pltpu.SemaphoreType.DMA],
        name="split_pixels",
    )(frames)


def coherence_kernel(total_pixels, edges_ref, parts_ref, out_ref):
    own = lax.axis_index("tm")
    count = jnp.full((TAPERS, LANES), edges_ref[own + 1] - edges_ref[own], jnp.int32).astype(jnp.float32)
    scale = jnp.sqrt(count * jnp.float32(total_pixels))
    total = jnp.sum(parts_ref[...], axis=0, keepdims=True)
    lane = lax.broadcasted_iota(jnp.int32, (TAPERS, LANES), 1)
    row = lax.broadcasted_iota(jnp.int32, (TAPERS, LANES), 0)
    value = jnp.where(jnp.right_shift(lane, 4) == row, jnp.broadcast_to(total, (TAPERS, LANES)), 0.0)
    for shift in (16, 32, 64):
        value = value + pltpu.roll(value, shift, 1)
    diag = jnp.where(jnp.bitwise_and(lane, TAPERS * 2 - 1) == row, value, 0.0)
    diag = jnp.where(lane < TAPERS, diag, 0.0)
    power_row = jnp.sum(diag, axis=1, keepdims=True) + 1e-06
    power_lane = jnp.sum(diag, axis=0, keepdims=True)
    power_lane = jnp.where(lane < TAPERS, power_lane, pltpu.roll(jnp.broadcast_to(power_lane, (TAPERS, LANES)), TAPERS, 1)) + 1e-06
    denominator = jnp.sqrt(power_row * power_lane)
    off = jnp.bitwise_and(lane, TAPERS - 1) != row
    result = jnp.where(off, value * scale / denominator, 0.0)
    out_ref[0, 0] = result[:, :TAPERS]
    out_ref[0, 1] = result[:, TAPERS : 2 * TAPERS]


def coherence_of(band_edges, parts, total_pixels):
    return pl.pallas_call(
        functools.partial(coherence_kernel, total_pixels),
        out_shape=jax.ShapeDtypeStruct((1, 2, TAPERS, TAPERS), jnp.float32),
        in_specs=[pl.BlockSpec(memory_space=pltpu.SMEM), pl.BlockSpec(memory_space=pltpu.VMEM)],
        name="coherence",
    )(band_edges, parts)


def local(frames, band_edges):
    groups = lax.axis_size("tm")
    n_pix = lax.axis_size("pix")
    pix_dev = frames.shape[1]
    share = pix_dev // groups
    blocks = split_pixels(frames, groups)
    data = lax.all_to_all(blocks, "tm", 0, 0, tiled=True).reshape(NT, share)
    waves = base_waves()
    bin_ids = jnp.arange(NB + 1, dtype=jnp.int32)
    band_of = jnp.sum((bin_ids[:, None] >= band_edges[None, 1:]).astype(jnp.int32), axis=1)
    keep = 1.0 - jnp.any(bin_ids[:, None] == band_edges[None, :], axis=1).astype(jnp.float32)
    sums = band_sums_of(data, waves, band_of, keep, n_pix)
    parts = lax.all_to_all(sums.reshape(groups * n_pix, 1, LANES), ("pix", "tm"), 0, 0, tiled=True)
    return coherence_of(band_edges, parts.reshape(groups * n_pix, LANES), pix_dev * n_pix)


def solution(mesh):
    return jax.shard_map(
        local,
        mesh=mesh,
        in_specs=(P("tm", "pix"), P()),
        out_specs=P("tm", None, None, None),
        check_vma=False,
    )
```
